32 devices in a mesh: grp: 2 (over y), tm: 4 (over z), sub: 2 (over x), ch: 2 (over core).
Axes of the slice: x: 2, y: 2, z: 4, core: 2. Of those that a mesh axis runs over, the one named last changes fastest.
Arguments:
- archive: float32 [16, 16384], P('ch', ('grp', 'tm')), parts along dimension 1, may hold values from -6 to 6
- tail: float32 [16, 254], P(None, 'grp'), parts along dimension 1, may hold values from -6 to 6
- precision: float32 [16, 16], replicated, may hold values from -1.5 to 1.5
- tile_list: int32 [8, 2, 2, 2], P(('grp', 'tm'), 'sub'), parts along dimension 0, may hold values from 0 to 15, as said below
Outputs:
- profile: float32 [16384], P(('grp', 'tm', 'sub')), parts along dimension 0
The draws below stay inside these ranges and needn't reach their ends.
There are 2 independent parts, one for each index of `grp`. The reference program is written for one: setup_inputs(seed, part) draws one part's arguments, and reference() takes and returns one part's arrays. A program takes and returns all parts, laid end to end along the dimension named above; an argument that names none is the same for every part. Nothing has to cross between parts.
Inputs may be any that keep to these rules, and one draw needn't show every extreme that they name: `tile_list`: each pair has row block <= column block; every block k < 16 appears in some pair; pairs may repeat.
All inputs are finite; a program needn't handle non-finite values.
Results may differ from the reference program's by a relative error of at most 0.0003.
Values may be sent and summed in bfloat16 or wider, within the bound.
A program may use at most 128 MiB of HBM per device.

```python
import jax
import jax.numpy as jnp
from jax import lax

C = 16
M = 128
TS = 512
SLOTS = 2
DEPTH = 2048
EXCL = 32
NB = 16
NS = 8192
N_TM = 4
N_SUB = 2


def draw_tile_list(key, part):
    slot_count = N_TM * N_SUB * SLOTS
    order_blocks = jax.random.permutation(jax.random.fold_in(key, 11), NB).astype(jnp.int32)
    if NB % 2 == 1:
        order_blocks = jnp.concatenate([order_blocks, order_blocks[-1:]])
    first = order_blocks[0::2]
    second = order_blocks[1::2]
    covering = first.shape[0]
    extra_first = jax.random.randint(jax.random.fold_in(key, 13), (slot_count - covering,), 0, NB).astype(jnp.int32)
    extra_second = jax.random.randint(jax.random.fold_in(key, 17), (slot_count - covering,), 0, NB).astype(jnp.int32)
    left = jnp.concatenate([first, extra_first])
    right = jnp.concatenate([second, extra_second])
    lower = jnp.minimum(left, right)
    upper = jnp.maximum(left, right)
    shuffle = jax.random.permutation(jax.random.fold_in(key, 23), slot_count)
    pairs_out = jnp.stack([lower[shuffle], upper[shuffle]], axis=-1)
    return pairs_out.reshape(N_TM, N_SUB, SLOTS, 2).astype(jnp.int32)


def levels(rng, extent, shards, low, largest):
    def one(position, shards_of):
        steps = jax.random.uniform(jax.random.fold_in(jax.random.fold_in(rng, 6), position), (shards_of,), jnp.float32, low / len(shards), largest / len(shards))
        return jnp.repeat(jnp.exp(steps), extent[position] // shards_of).reshape((-1,) + (1,) * (len(extent) - position - 1))

    loudness = one(*shards[0])
    for cut in shards[1:]:
        loudness = loudness * one(*cut)
    return loudness


def normal_values(key, dims, spread, bound, shards=(), kind=jnp.bfloat16):
    values = spread * jax.random.normal(key, dims, jnp.float32)
    if shards:
        values = values * levels(key, dims, shards, -0.22, 0.18)
    return jnp.clip(values, -bound, bound).astype(kind)


def setup_inputs(seed: int = 0, part: int = 0) -> dict:
    streams_of = jax.random.split(jax.random.key(seed), 5)
    own_keys = jax.random.split(jax.random.fold_in(streams_of[4], part), 5)
    return {
        "archive": normal_values(own_keys[0], (C, NS), 1.0, 6.0, ((0, 2), (1, 4)), jnp.float32),
        "tail": normal_values(own_keys[1], (C, M - 1), 1.0, 6.0, (), jnp.float32),
        "precision": normal_values(streams_of[2], (C, C), C ** -0.5, 1.5, (), jnp.float32),
        "tile_list": draw_tile_list(jax.random.fold_in(jax.random.fold_in(streams_of[4], part), 71), part),
    }


def whiten(factor, samples):
    return jnp.dot(factor, samples, precision=lax.Precision.HIGHEST, preferred_element_type=jnp.float32).astype(jnp.bfloat16)


def build_rows(series_wide, start):
    segment = lax.dynamic_slice_in_dim(series_wide, start, TS + M - 1, 1)
    return jnp.stack([segment[:, offset:offset + TS] for offset in range(M)]).reshape(M * C, TS)


def lower_into(profile, values, start):
    current = lax.dynamic_slice_in_dim(profile, start, values.shape[0])
    return lax.dynamic_update_slice_in_dim(profile, jnp.minimum(current, values), start, 0)


def reference(archive, tail, precision, tile_list):
    series = jnp.concatenate([whiten(precision, archive), whiten(precision, tail)], axis=1)
    series_wide = series.astype(jnp.float32)
    squares = jnp.sum(series_wide * series_wide, axis=0)
    window_norms = lax.reduce_window(squares, jnp.array(0, squares.dtype), lax.add, (M,), (1,), "VALID")
    tile_pairs = tile_list.reshape(-1, 2).astype(jnp.int32)

    def one_pair(profile, pair):
        row_start = (pair[0] * TS).astype(jnp.int32)
        col_start = (pair[1] * TS).astype(jnp.int32)
        row_hankel = build_rows(series_wide, row_start)
        col_hankel = build_rows(series_wide, col_start)
        products = jnp.dot(row_hankel.T, col_hankel, precision=lax.Precision.HIGHEST)
        row_norms = lax.dynamic_slice_in_dim(window_norms, row_start, TS)
        col_norms = lax.dynamic_slice_in_dim(window_norms, col_start, TS)
        distance = (row_norms[:, None] + col_norms[None, :] - 2.0 * products) / DEPTH
        row_index = row_start + jnp.arange(TS).astype(jnp.int32)
        col_index = col_start + jnp.arange(TS).astype(jnp.int32)
        too_near = jnp.abs(row_index[:, None] - col_index[None, :]) < EXCL
        distance = jnp.where(too_near, jnp.inf, distance)
        profile = lower_into(profile, jnp.min(distance, axis=1), row_start)
        profile = lower_into(profile, jnp.min(distance, axis=0), col_start)
        return profile, None

    start_profile = jnp.full((NS,), jnp.inf, jnp.float32)
    profile, unused = lax.scan(one_pair, start_profile, tile_pairs)
    return profile
```

```python
import functools

import jax
import jax.numpy as jnp
from jax import lax
from jax.experimental import pallas as pl
from jax.experimental.pallas import tpu as pltpu
from jax.sharding import PartitionSpec as P

M = 128
TS = 512
SLOTS = 2
DEPTH = 2048
EXCL = 32
LANES = 128
STEP = 16
COLS = TS + M
ROWS = TS // 2 + M
SPAN = COLS + ROWS
MESH = pl.DeviceIdType.MESH


def whiten(factor, samples):
    return jnp.dot(
        factor, samples, precision=lax.Precision.HIGHEST, preferred_element_type=jnp.float32
    ).astype(jnp.bfloat16)


def kernel(
    n_tm,
    n_sub,
    tiles_ref,
    archive_ref,
    tail_ref,
    precision_ref,
    out_ref,
    raw_ref,
    series_ref,
    hankel_ref,
    lagged_ref,
    mine_ref,
    theirs_ref,
    raw_sems,
    time_send,
    time_recv,
    pair_send,
    pair_recv,
    min_sems,
):
    tm, sub, ch = lax.axis_index("tm"), lax.axis_index("sub"), lax.axis_index("ch")
    other = 1 - ch
    group = n_tm * n_sub * 2
    me = (tm * n_sub + sub) * 2 + ch
    channels, span = archive_ref.shape
    half = span // 2
    starts_all = n_tm * span

    def place(rank):
        owner = rank // 2
        return {"tm": owner // n_sub, "sub": owner % n_sub, "ch": rank % 2}

    def each_peer(action):
        if group <= 16:
            for step in range(1, group):
                action(step)
        else:
            lax.fori_loop(1, group, lambda step, _: (action(step), 0)[1], 0)

    barrier = pltpu.get_barrier_semaphore()
    each_peer(
        lambda step: pl.semaphore_signal(
            barrier, inc=1, device_id=place(lax.rem(me + step, group)), device_id_type=MESH
        )
    )
    own_rows = pl.ds(pl.multiple_of(ch * channels, channels), channels)
    raw_ref[own_rows, :] = archive_ref[:, pl.ds(pl.multiple_of(ch * half, half), half)]
    factor = precision_ref[...]
    last = starts_all // LANES
    series_ref[last] = jnp.zeros((2 * channels, LANES), jnp.bfloat16)
    series_ref[last, :, : M - 1] = whiten(factor, tail_ref[...])
    pl.semaphore_wait(barrier, group - 1)

    swap = pltpu.make_async_remote_copy(
        src_ref=archive_ref.at[:, pl.ds(pl.multiple_of(other * half, half), half)],
        dst_ref=raw_ref.at[own_rows, :],
        send_sem=raw_sems.at[0],
        recv_sem=raw_sems.at[1],
        device_id={"ch": other},
        device_id_type=MESH,
    )
    swap.start()
    swap.wait_recv()

    tiles = half // LANES

    def chunk(owner, part):
        return series_ref.at[pl.ds((owner * 2 + part) * tiles, tiles)]

    mine = chunk(tm, ch)
    whitened = whiten(factor, raw_ref[...])
    for k in range(tiles):
        series_ref[(tm * 2 + ch) * tiles + k] = whitened[:, k * LANES : (k + 1) * LANES]
    along_time = [None]
    for back in range(1, n_tm):
        along_time.append(
            pltpu.make_async_remote_copy(
                src_ref=mine,
                dst_ref=mine,
                send_sem=time_send.at[back],
                recv_sem=time_recv.at[back],
                device_id={"tm": lax.rem(tm + back, n_tm)},
                device_id_type=MESH,
            )
        )
        along_time[back].start()
    to_pair = []
    for back in range(n_tm):
        if back:
            along_time[back].wait_recv()
        held = chunk(lax.rem(tm + n_tm - back, n_tm), ch)
        to_pair.append(
            pltpu.make_async_remote_copy(
                src_ref=held,
                dst_ref=held,
                send_sem=pair_send.at[back],
                recv_sem=pair_recv.at[back],
                device_id={"ch": other},
                device_id_type=MESH,
            )
        )
        to_pair[back].start()
    for copy in to_pair:
        copy.wait_recv()

    pieces = []
    for slot in range(SLOTS):
        per_block = TS // LANES
        row_tile = tiles_ref[0, 0, slot, 0] * per_block + ch * (per_block // 2)
        col_tile = tiles_ref[0, 0, slot, 1] * per_block
        pieces.extend(series_ref[col_tile + k] for k in range(COLS // LANES))
        pieces.extend(series_ref[row_tile + k] for k in range(ROWS // LANES))
    segment = jnp.concatenate(pieces, axis=1).astype(jnp.float32)
    width = segment.shape[1]
    depth = segment.shape[0]
    for lag in range(STEP):
        moved = segment if lag == 0 else pltpu.roll(segment, width - lag, axis=1)
        hankel_ref[lag * depth : (lag + 1) * depth, :] = moved.astype(jnp.bfloat16)
    size = STEP * depth
    unit = (
        lax.broadcasted_iota(jnp.int32, (size, size), 0)
        == lax.broadcasted_iota(jnp.int32, (size, size), 1)
    ).astype(jnp.bfloat16)
    for at in range(0, width, size):
        lagged_ref[at : at + size, :] = lax.dot_general(
            unit,
            hankel_ref[:, at : at + size],
            (((1,), (1,)), ((), ())),
            preferred_element_type=jnp.float32,
        ).astype(jnp.bfloat16)
    norms = jnp.broadcast_to(jnp.sum(segment * segment, axis=0, keepdims=True), (8, width))
    shift = 1
    while shift < M:
        norms = norms + pltpu.roll(norms, width - shift, axis=1)
        shift *= 2

    owners, piece_rows, _ = mine_ref.shape
    place_shape = (owners, piece_rows, LANES)
    line = lax.broadcasted_iota(jnp.int32, place_shape, 0) * piece_rows
    line = line + lax.broadcasted_iota(jnp.int32, place_shape, 1)
    block_of, part_of = line // per_block, line % per_block
    best = jnp.full(place_shape, jnp.inf, jnp.float32)
    for slot in range(SLOTS):
        col_at = slot * SPAN
        row_at = col_at + COLS
        n_rows = TS // 2
        left = jnp.concatenate(
            [lagged_ref[row_at + v : row_at + v + n_rows, :] for v in range(0, M, STEP)], axis=1
        )
        right = jnp.concatenate(
            [lagged_ref[col_at + v : col_at + v + TS, :] for v in range(0, M, STEP)], axis=1
        )
        products = lax.dot_general(
            left, right, (((1,), (1,)), ((), ())), preferred_element_type=jnp.float32
        )
        row_block = tiles_ref[0, 0, slot, 0]
        col_block = tiles_ref[0, 0, slot, 1]
        between = row_block * TS + ch * n_rows - col_block * TS
        separation = (
            lax.broadcasted_iota(jnp.int32, (n_rows, TS), 0)
            - lax.broadcasted_iota(jnp.int32, (n_rows, TS), 1)
            + between
        )
        scores = jnp.where(jnp.abs(separation) < EXCL, jnp.inf, -2.0 * products)
        row_norms = norms[:1, row_at : row_at + n_rows]
        col_norms = norms[:1, col_at : col_at + TS]
        row_wide = jnp.transpose(jnp.broadcast_to(row_norms, (LANES, n_rows)))
        by_col = jnp.min(scores + jnp.concatenate([row_wide] * per_block, axis=1), axis=0, keepdims=True)
        by_col = (by_col + col_norms) * (1.0 / DEPTH)
        with_col = scores + col_norms
        folded = with_col[:, :LANES]
        for q in range(1, per_block):
            folded = jnp.minimum(folded, with_col[:, q * LANES : (q + 1) * LANES])
        by_row = jnp.min(jnp.transpose(folded), axis=0, keepdims=True)
        by_row = (by_row + row_norms) * (1.0 / DEPTH)
        for q in range(per_block):
            here = by_col[:, q * LANES : (q + 1) * LANES].reshape(1, 1, LANES)
            hit = (block_of == col_block) & (part_of == q)
            best = jnp.minimum(best, jnp.where(hit, here, jnp.inf))
        for q in range(per_block // 2):
            here = by_row[:, q * LANES : (q + 1) * LANES].reshape(1, 1, LANES)
            hit = (block_of == row_block) & (part_of == q + ch * (per_block // 2))
            best = jnp.minimum(best, jnp.where(hit, here, jnp.inf))
    mine_ref[...] = best

    def send_minima(step):
        rank = lax.rem(me + step, group)
        pltpu.make_async_remote_copy(
            src_ref=mine_ref.at[rank // 2],
            dst_ref=theirs_ref.at[step - 1],
            send_sem=min_sems.at[0],
            recv_sem=min_sems.at[1],
            device_id=place(rank),
            device_id_type=MESH,
        ).start()

    each_peer(send_minima)
    every = pltpu.make_async_remote_copy(
        src_ref=theirs_ref,
        dst_ref=theirs_ref,
        send_sem=min_sems.at[0],
        recv_sem=min_sems.at[1],
        device_id={"ch": other},
        device_id_type=MESH,
    )
    every.wait_recv()
    out_ref[...] = jnp.minimum(mine_ref[me // 2], jnp.min(theirs_ref[...], axis=0))
    every.wait_send()
    swap.wait_send()
    for copy in along_time[1:] + to_pair:
        copy.wait_send()


def body(archive, tail, precision, tile_list):
    n_tm, n_sub = lax.axis_size("tm"), lax.axis_size("sub")
    group = n_tm * n_sub * 2
    channels, span = archive.shape
    starts_all = span * n_tm
    piece_rows = starts_all // (n_tm * n_sub) // LANES
    every = 2 * channels
    width = SLOTS * SPAN
    vmem = pl.BlockSpec(memory_space=pltpu.VMEM)
    out = pl.pallas_call(
        functools.partial(kernel, n_tm, n_sub),
        out_shape=jax.ShapeDtypeStruct((piece_rows, LANES), jnp.float32),
        in_specs=[pl.BlockSpec(memory_space=pltpu.SMEM), vmem, vmem, vmem],
        out_specs=vmem,
        scratch_shapes=[
            pltpu.VMEM((every, span // 2), jnp.float32),
            pltpu.VMEM((starts_all // LANES + 1, every, LANES), jnp.bfloat16),
            pltpu.VMEM((STEP * every, width), jnp.bfloat16),
            pltpu.VMEM((width, STEP * every), jnp.bfloat16),
            pltpu.VMEM((n_tm * n_sub, piece_rows, LANES), jnp.float32),
            pltpu.VMEM((group - 1, piece_rows, LANES), jnp.float32),
            pltpu.SemaphoreType.DMA((2,)),
            pltpu.SemaphoreType.DMA((n_tm,)),
            pltpu.SemaphoreType.DMA((n_tm,)),
            pltpu.SemaphoreType.DMA((n_tm,)),
            pltpu.SemaphoreType.DMA((n_tm,)),
            pltpu.SemaphoreType.DMA((2,)),
        ],
        compiler_params=pltpu.CompilerParams(
            collective_id=0, has_side_effects=True, vmem_limit_bytes=40 * 2**20
        ),
    )(tile_list, archive, tail, precision)
    return out.reshape(-1)


def solution(mesh):
    placed = (P("ch", ("grp", "tm")), P(None, "grp"), P(), P(("grp", "tm"), "sub", None, None))
    return jax.shard_map(
        body, mesh=mesh, in_specs=placed, out_specs=P(("grp", "tm", "sub")), check_vma=False
    )
```

```python
import functools

import jax
import jax.numpy as jnp
from jax import lax
from jax.experimental import pallas as pl
from jax.experimental.pallas import tpu as pltpu
from jax.sharding import PartitionSpec as P

M = 128
TS = 512
SLOTS = 2
DEPTH = 2048
EXCL = 32
LANES = 128
STEP = 16
COLS = TS + M
ROWS = TS // 2 + M
SPAN = COLS + ROWS
MESH = pl.DeviceIdType.MESH


def whiten(factor, samples):
    return jnp.dot(
        factor, samples, precision=lax.Precision.HIGHEST, preferred_element_type=jnp.float32
    ).astype(jnp.bfloat16)


def kernel(
    n_tm,
    n_sub,
    tiles_hbm,
    archive_ref,
    tail_hbm,
    precision_hbm,
    out_ref,
    tiles_ref,
    tail_ref,
    precision_ref,
    raw_ref,
    series_ref,
    hankel_ref,
    lagged_ref,
    mine_ref,
    theirs_ref,
    load_sems,
    raw_sems,
    time_send,
    time_recv,
    pair_send,
    pair_recv,
    min_sems,
):
    tm, sub, ch = lax.axis_index("tm"), lax.axis_index("sub"), lax.axis_index("ch")
    other = 1 - ch
    group = n_tm * n_sub * 2
    me = (tm * n_sub + sub) * 2 + ch
    channels, span = archive_ref.shape
    half = span // 2
    starts_all = n_tm * span

    def place(rank):
        owner = rank // 2
        return {"tm": owner // n_sub, "sub": owner % n_sub, "ch": rank % 2}

    def each_peer(action):
        if group <= 16:
            for step in range(1, group):
                action(step)
        else:
            lax.fori_loop(1, group, lambda step, _: (action(step), 0)[1], 0)

    own_rows = pl.ds(pl.multiple_of(ch * channels, channels), channels)
    own_half = archive_ref.at[:, pl.ds(pl.multiple_of(ch * half, half), half)]
    loads = [
        pltpu.make_async_copy(source, target, load_sems.at[at])
        for at, (source, target) in enumerate(
            (
                (precision_hbm, precision_ref),
                (tail_hbm, tail_ref),
                (own_half, raw_ref.at[own_rows, :]),
                (tiles_hbm, tiles_ref),
            )
        )
    ]
    for load in loads:
        load.start()
    barrier = pltpu.get_barrier_semaphore()
    each_peer(
        lambda step: pl.semaphore_signal(
            barrier, inc=1, device_id=place(lax.rem(me + step, group)), device_id_type=MESH
        )
    )
    for load in loads[:2]:
        load.wait()
    factor = precision_ref[...]
    last = starts_all // LANES
    series_ref[last] = jnp.zeros((2 * channels, LANES), jnp.bfloat16)
    series_ref[last, :, : M - 1] = whiten(factor, tail_ref[...])
    pl.semaphore_wait(barrier, group - 1)

    swap = pltpu.make_async_remote_copy(
        src_ref=archive_ref.at[:, pl.ds(pl.multiple_of(other * half, half), half)],
        dst_ref=raw_ref.at[own_rows, :],
        send_sem=raw_sems.at[0],
        recv_sem=raw_sems.at[1],
        device_id={"ch": other},
        device_id_type=MESH,
    )
    swap.start()
    for load in loads[2:]:
        load.wait()
    swap.wait_recv()

    tiles = half // LANES

    def chunk(owner, part):
        return series_ref.at[pl.ds((owner * 2 + part) * tiles, tiles)]

    mine = chunk(tm, ch)
    whitened = whiten(factor, raw_ref[...])
    for k in range(tiles):
        series_ref[(tm * 2 + ch) * tiles + k] = whitened[:, k * LANES : (k + 1) * LANES]
    along_time = [None]
    for back in range(1, n_tm):
        along_time.append(
            pltpu.make_async_remote_copy(
                src_ref=mine,
                dst_ref=mine,
                send_sem=time_send.at[back],
                recv_sem=time_recv.at[back],
                device_id={"tm": lax.rem(tm + back, n_tm)},
                device_id_type=MESH,
            )
        )
        along_time[back].start()
    to_pair = []
    for back in range(n_tm):
        if back:
            along_time[back].wait_recv()
        held = chunk(lax.rem(tm + n_tm - back, n_tm), ch)
        to_pair.append(
            pltpu.make_async_remote_copy(
                src_ref=held,
                dst_ref=held,
                send_sem=pair_send.at[back],
                recv_sem=pair_recv.at[back],
                device_id={"ch": other},
                device_id_type=MESH,
            )
        )
        to_pair[back].start()
    for copy in to_pair:
        copy.wait_recv()

    pieces = []
    for slot in range(SLOTS):
        per_block = TS // LANES
        row_tile = tiles_ref[0, 0, slot, 0] * per_block + ch * (per_block // 2)
        col_tile = tiles_ref[0, 0, slot, 1] * per_block
        pieces.extend(series_ref[col_tile + k] for k in range(COLS // LANES))
        pieces.extend(series_ref[row_tile + k] for k in range(ROWS // LANES))
    segment = jnp.concatenate(pieces, axis=1).astype(jnp.float32)
    width = segment.shape[1]
    depth = segment.shape[0]
    for lag in range(STEP):
        moved = segment if lag == 0 else pltpu.roll(segment, width - lag, axis=1)
        hankel_ref[lag * depth : (lag + 1) * depth, :] = moved.astype(jnp.bfloat16)
    size = STEP * depth
    unit = (
        lax.broadcasted_iota(jnp.int32, (size, size), 0)
        == lax.broadcasted_iota(jnp.int32, (size, size), 1)
    ).astype(jnp.bfloat16)
    for at in range(0, width, size):
        lagged_ref[at : at + size, :] = lax.dot_general(
            unit,
            hankel_ref[:, at : at + size],
            (((1,), (1,)), ((), ())),
            preferred_element_type=jnp.float32,
        ).astype(jnp.bfloat16)
    norms = jnp.broadcast_to(jnp.sum(segment * segment, axis=0, keepdims=True), (8, width))
    shift = 1
    while shift < M:
        norms = norms + pltpu.roll(norms, width - shift, axis=1)
        shift *= 2

    owners, piece_rows, _ = mine_ref.shape
    place_shape = (owners, piece_rows, LANES)
    line = lax.broadcasted_iota(jnp.int32, place_shape, 0) * piece_rows
    line = line + lax.broadcasted_iota(jnp.int32, place_shape, 1)
    block_of, part_of = line // per_block, line % per_block
    best = jnp.full(place_shape, jnp.inf, jnp.float32)
    for slot in range(SLOTS):
        col_at = slot * SPAN
        row_at = col_at + COLS
        n_rows = TS // 2
        left = jnp.concatenate(
            [lagged_ref[row_at + v : row_at + v + n_rows, :] for v in range(0, M, STEP)], axis=1
        )
        right = jnp.concatenate(
            [lagged_ref[col_at + v : col_at + v + TS, :] for v in range(0, M, STEP)], axis=1
        )
        products = lax.dot_general(
            left, right, (((1,), (1,)), ((), ())), preferred_element_type=jnp.float32
        )
        row_block = tiles_ref[0, 0, slot, 0]
        col_block = tiles_ref[0, 0, slot, 1]
        between = row_block * TS + ch * n_rows - col_block * TS
        separation = (
            lax.broadcasted_iota(jnp.int32, (n_rows, TS), 0)
            - lax.broadcasted_iota(jnp.int32, (n_rows, TS), 1)
            + between
        )
        scores = jnp.where(jnp.abs(separation) < EXCL, jnp.inf, -2.0 * products)
        row_norms = norms[:1, row_at : row_at + n_rows]
        col_norms = norms[:1, col_at : col_at + TS]
        row_wide = jnp.transpose(jnp.broadcast_to(row_norms, (LANES, n_rows)))
        by_col = jnp.min(scores + jnp.concatenate([row_wide] * per_block, axis=1), axis=0, keepdims=True)
        by_col = (by_col + col_norms) * (1.0 / DEPTH)
        with_col = scores + col_norms
        folded = with_col[:, :LANES]
        for q in range(1, per_block):
            folded = jnp.minimum(folded, with_col[:, q * LANES : (q + 1) * LANES])
        by_row = jnp.min(jnp.transpose(folded), axis=0, keepdims=True)
        by_row = (by_row + row_norms) * (1.0 / DEPTH)
        for q in range(per_block):
            here = by_col[:, q * LANES : (q + 1) * LANES].reshape(1, 1, LANES)
            hit = (block_of == col_block) & (part_of == q)
            best = jnp.minimum(best, jnp.where(hit, here, jnp.inf))
        for q in range(per_block // 2):
            here = by_row[:, q * LANES : (q + 1) * LANES].reshape(1, 1, LANES)
            hit = (block_of == row_block) & (part_of == q + ch * (per_block // 2))
            best = jnp.minimum(best, jnp.where(hit, here, jnp.inf))
    mine_ref[...] = best

    def send_minima(step):
        rank = lax.rem(me + step, group)
        pltpu.make_async_remote_copy(
            src_ref=mine_ref.at[rank // 2],
            dst_ref=theirs_ref.at[step - 1],
            send_sem=min_sems.at[0],
            recv_sem=min_sems.at[1],
            device_id=place(rank),
            device_id_type=MESH,
        ).start()

    each_peer(send_minima)
    every = pltpu.make_async_remote_copy(
        src_ref=theirs_ref,
        dst_ref=theirs_ref,
        send_sem=min_sems.at[0],
        recv_sem=min_sems.at[1],
        device_id={"ch": other},
        device_id_type=MESH,
    )
    every.wait_recv()
    out_ref[...] = jnp.minimum(mine_ref[me // 2], jnp.min(theirs_ref[...], axis=0))
    every.wait_send()
    swap.wait_send()
    for copy in along_time[1:] + to_pair:
        copy.wait_send()


def body(archive, tail, precision, tile_list):
    n_tm, n_sub = lax.axis_size("tm"), lax.axis_size("sub")
    group = n_tm * n_sub * 2
    channels, span = archive.shape
    starts_all = span * n_tm
    piece_rows = starts_all // (n_tm * n_sub) // LANES
    every = 2 * channels
    width = SLOTS * SPAN
    anywhere = pl.BlockSpec(memory_space=pl.ANY)
    out = pl.pallas_call(
        functools.partial(kernel, n_tm, n_sub),
        out_shape=jax.ShapeDtypeStruct((piece_rows, LANES), jnp.float32),
        in_specs=[anywhere] * 4,
        out_specs=pl.BlockSpec(memory_space=pltpu.VMEM),
        scratch_shapes=[
            pltpu.SMEM(tile_list.shape, jnp.int32),
            pltpu.VMEM(tail.shape, jnp.float32),
            pltpu.VMEM(precision.shape, jnp.float32),
            pltpu.VMEM((every, span // 2), jnp.float32),
            pltpu.VMEM((starts_all // LANES + 1, every, LANES), jnp.bfloat16),
            pltpu.VMEM((STEP * every, width), jnp.bfloat16),
            pltpu.VMEM((width, STEP * every), jnp.bfloat16),
            pltpu.VMEM((n_tm * n_sub, piece_rows, LANES), jnp.float32),
            pltpu.VMEM((group - 1, piece_rows, LANES), jnp.float32),
            pltpu.SemaphoreType.DMA((4,)),
            pltpu.SemaphoreType.DMA((2,)),
            pltpu.SemaphoreType.DMA((n_tm,)),
            pltpu.SemaphoreType.DMA((n_tm,)),
            pltpu.SemaphoreType.DMA((n_tm,)),
            pltpu.SemaphoreType.DMA((n_tm,)),
            pltpu.SemaphoreType.DMA((2,)),
        ],
        compiler_params=pltpu.CompilerParams(
            collective_id=0, has_side_effects=True, vmem_limit_bytes=60 * 2**20
        ),
    )(tile_list, archive, tail, precision)
    return out.reshape(-1)


def solution(mesh):
    placed = (P("ch", ("grp", "tm")), P(None, "grp"), P(), P(("grp", "tm"), "sub", None, None))
    return jax.shard_map(
        body, mesh=mesh, in_specs=placed, out_specs=P(("grp", "tm", "sub")), check_vma=False
    )
```

```python
import functools

import jax
import jax.numpy as jnp
from jax import lax
from jax.experimental import pallas as pl
from jax.experimental.pallas import tpu as pltpu
from jax.sharding import PartitionSpec as P

M = 128
TS = 512
SLOTS = 2
DEPTH = 2048
EXCL = 32
LANES = 128
STEP = 16
COLS = TS + M
ROWS = TS // 2 + M
SPAN = COLS + ROWS
MESH = pl.DeviceIdType.MESH


def whiten(factor, samples):
    return jnp.dot(
        factor, samples, precision=lax.Precision.HIGHEST, preferred_element_type=jnp.float32
    ).astype(jnp.bfloat16)


def kernel(
    n_tm,
    n_sub,
    tiles_hbm,
    archive_ref,
    tail_hbm,
    precision_hbm,
    out_ref,
    tiles_ref,
    tail_ref,
    precision_ref,
    raw_ref,
    series_ref,
    hankel_ref,
    lagged_ref,
    mine_ref,
    theirs_ref,
    load_sems,
    raw_sems,
    time_send,
    time_recv,
    pair_send,
    pair_recv,
    min_sems,
):
    tm, sub, ch = lax.axis_index("tm"), lax.axis_index("sub"), lax.axis_index("ch")
    other = 1 - ch
    group = n_tm * n_sub * 2
    me = (tm * n_sub + sub) * 2 + ch
    channels, span = archive_ref.shape
    half = span // 2
    starts_all = n_tm * span

    def crossed(a, b, count):
        total, bit = 0, 1
        while bit < count:
            total = total + lax.rem(a // bit + b // bit, 2) * bit
            bit *= 2
        return total

    def place(rank):
        owner = rank // 2
        return {"tm": owner // n_sub, "sub": owner % n_sub, "ch": rank % 2}

    def each_peer(action):
        if group <= 16:
            for step in reversed(range(1, group)):
                action(step)
        else:
            lax.fori_loop(1, group, lambda step, _: (action(group - step), 0)[1], 0)

    own_rows = pl.ds(pl.multiple_of(ch * channels, channels), channels)
    own_half = archive_ref.at[:, pl.ds(pl.multiple_of(ch * half, half), half)]
    loads = [
        pltpu.make_async_copy(source, target, load_sems.at[at])
        for at, (source, target) in enumerate(
            (
                (precision_hbm, precision_ref),
                (tail_hbm, tail_ref),
                (own_half, raw_ref.at[own_rows, :]),
                (tiles_hbm, tiles_ref),
            )
        )
    ]
    for load in loads:
        load.start()
    barrier = pltpu.get_barrier_semaphore()
    each_peer(
        lambda step: pl.semaphore_signal(
            barrier, inc=1, device_id=place(crossed(me, step, group)), device_id_type=MESH
        )
    )
    for load in loads[:2]:
        load.wait()
    factor = precision_ref[...]
    last = starts_all // LANES
    series_ref[last] = jnp.zeros((2 * channels, LANES), jnp.bfloat16)
    series_ref[last, :, : M - 1] = whiten(factor, tail_ref[...])
    pl.semaphore_wait(barrier, group - 1)

    swap = pltpu.make_async_remote_copy(
        src_ref=archive_ref.at[:, pl.ds(pl.multiple_of(other * half, half), half)],
        dst_ref=raw_ref.at[own_rows, :],
        send_sem=raw_sems.at[0],
        recv_sem=raw_sems.at[1],
        device_id={"ch": other},
        device_id_type=MESH,
    )
    swap.start()
    for load in loads[2:]:
        load.wait()
    swap.wait_recv()

    tiles = half // LANES

    def chunk(owner, part):
        return series_ref.at[pl.ds((owner * 2 + part) * tiles, tiles)]

    mine = chunk(tm, ch)
    whitened = whiten(factor, raw_ref[...])
    for k in range(tiles):
        series_ref[(tm * 2 + ch) * tiles + k] = whitened[:, k * LANES : (k + 1) * LANES]
    along_time = [None] * n_tm
    for far in sorted(range(1, n_tm), key=lambda d: (d < n_tm // 2, d)):
        along_time[far] = pltpu.make_async_remote_copy(
            src_ref=mine,
            dst_ref=mine,
            send_sem=time_send.at[far],
            recv_sem=time_recv.at[far],
            device_id={"tm": crossed(tm, far, n_tm)},
            device_id_type=MESH,
        )
        along_time[far].start()
    to_pair = []
    for far in range(n_tm):
        if far:
            along_time[far].wait_recv()
        held = chunk(crossed(tm, far, n_tm), ch)
        to_pair.append(
            pltpu.make_async_remote_copy(
                src_ref=held,
                dst_ref=held,
                send_sem=pair_send.at[far],
                recv_sem=pair_recv.at[far],
                device_id={"ch": other},
                device_id_type=MESH,
            )
        )
        to_pair[far].start()
    for copy in to_pair:
        copy.wait_recv()

    pieces = []
    for slot in range(SLOTS):
        per_block = TS // LANES
        row_tile = tiles_ref[0, 0, slot, 0] * per_block + ch * (per_block // 2)
        col_tile = tiles_ref[0, 0, slot, 1] * per_block
        pieces.extend(series_ref[col_tile + k] for k in range(COLS // LANES))
        pieces.extend(series_ref[row_tile + k] for k in range(ROWS // LANES))
    segment = jnp.concatenate(pieces, axis=1).astype(jnp.float32)
    width = segment.shape[1]
    depth = segment.shape[0]
    for lag in range(STEP):
        moved = segment if lag == 0 else pltpu.roll(segment, width - lag, axis=1)
        hankel_ref[lag * depth : (lag + 1) * depth, :] = moved.astype(jnp.bfloat16)
    size = STEP * depth
    unit = (
        lax.broadcasted_iota(jnp.int32, (size, size), 0)
        == lax.broadcasted_iota(jnp.int32, (size, size), 1)
    ).astype(jnp.bfloat16)
    for at in range(0, width, size):
        lagged_ref[at : at + size, :] = lax.dot_general(
            unit,
            hankel_ref[:, at : at + size],
            (((1,), (1,)), ((), ())),
            preferred_element_type=jnp.float32,
        ).astype(jnp.bfloat16)
    norms = jnp.broadcast_to(jnp.sum(segment * segment, axis=0, keepdims=True), (8, width))
    shift = 1
    while shift < M:
        norms = norms + pltpu.roll(norms, width - shift, axis=1)
        shift *= 2

    owners, piece_rows, _ = mine_ref.shape
    place_shape = (owners, piece_rows, LANES)
    line = lax.broadcasted_iota(jnp.int32, place_shape, 0) * piece_rows
    line = line + lax.broadcasted_iota(jnp.int32, place_shape, 1)
    block_of, part_of = line // per_block, line % per_block
    best = jnp.full(place_shape, jnp.inf, jnp.float32)
    for slot in range(SLOTS):
        col_at = slot * SPAN
        row_at = col_at + COLS
        n_rows = TS // 2
        left = jnp.concatenate(
            [lagged_ref[row_at + v : row_at + v + n_rows, :] for v in range(0, M, STEP)], axis=1
        )
        right = jnp.concatenate(
            [lagged_ref[col_at + v : col_at + v + TS, :] for v in range(0, M, STEP)], axis=1
        )
        products = lax.dot_general(
            left, right, (((1,), (1,)), ((), ())), preferred_element_type=jnp.float32
        )
        row_block = tiles_ref[0, 0, slot, 0]
        col_block = tiles_ref[0, 0, slot, 1]
        between = row_block * TS + ch * n_rows - col_block * TS
        separation = (
            lax.broadcasted_iota(jnp.int32, (n_rows, TS), 0)
            - lax.broadcasted_iota(jnp.int32, (n_rows, TS), 1)
            + between
        )
        scores = jnp.where(jnp.abs(separation) < EXCL, jnp.inf, -2.0 * products)
        row_norms = norms[:1, row_at : row_at + n_rows]
        col_norms = norms[:1, col_at : col_at + TS]
        row_wide = jnp.transpose(jnp.broadcast_to(row_norms, (LANES, n_rows)))
        by_col = jnp.min(scores + jnp.concatenate([row_wide] * per_block, axis=1), axis=0, keepdims=True)
        by_col = (by_col + col_norms) * (1.0 / DEPTH)
        with_col = scores + col_norms
        folded = with_col[:, :LANES]
        for q in range(1, per_block):
            folded = jnp.minimum(folded, with_col[:, q * LANES : (q + 1) * LANES])
        by_row = jnp.min(jnp.transpose(folded), axis=0, keepdims=True)
        by_row = (by_row + row_norms) * (1.0 / DEPTH)
        for q in range(per_block):
            here = by_col[:, q * LANES : (q + 1) * LANES].reshape(1, 1, LANES)
            hit = (block_of == col_block) & (part_of == q)
            best = jnp.minimum(best, jnp.where(hit, here, jnp.inf))
        for q in range(per_block // 2):
            here = by_row[:, q * LANES : (q + 1) * LANES].reshape(1, 1, LANES)
            hit = (block_of == row_block) & (part_of == q + ch * (per_block // 2))
            best = jnp.minimum(best, jnp.where(hit, here, jnp.inf))
    mine_ref[...] = best

    def send_minima(step):
        rank = crossed(me, step, group)
        pltpu.make_async_remote_copy(
            src_ref=mine_ref.at[rank // 2],
            dst_ref=theirs_ref.at[step - 1],
            send_sem=min_sems.at[0],
            recv_sem=min_sems.at[1],
            device_id=place(rank),
            device_id_type=MESH,
        ).start()

    each_peer(send_minima)
    every = pltpu.make_async_remote_copy(
        src_ref=theirs_ref,
        dst_ref=theirs_ref,
        send_sem=min_sems.at[0],
        recv_sem=min_sems.at[1],
        device_id={"ch": other},
        device_id_type=MESH,
    )
    every.wait_recv()
    out_ref[...] = jnp.minimum(mine_ref[me // 2], jnp.min(theirs_ref[...], axis=0))
    every.wait_send()
    swap.wait_send()
    for copy in along_time[1:] + to_pair:
        copy.wait_send()


def body(archive, tail, precision, tile_list):
    n_tm, n_sub = lax.axis_size("tm"), lax.axis_size("sub")
    group = n_tm * n_sub * 2
    channels, span = archive.shape
    starts_all = span * n_tm
    piece_rows = starts_all // (n_tm * n_sub) // LANES
    every = 2 * channels
    width = SLOTS * SPAN
    anywhere = pl.BlockSpec(memory_space=pl.ANY)
    out = pl.pallas_call(
        functools.partial(kernel, n_tm, n_sub),
        out_shape=jax.ShapeDtypeStruct((piece_rows, LANES), jnp.float32),
        in_specs=[anywhere] * 4,
        out_specs=pl.BlockSpec(memory_space=pltpu.VMEM),
        scratch_shapes=[
            pltpu.SMEM(tile_list.shape, jnp.int32),
            pltpu.VMEM(tail.shape, jnp.float32),
            pltpu.VMEM(precision.shape, jnp.float32),
            pltpu.VMEM((every, span // 2), jnp.float32),
            pltpu.VMEM((starts_all // LANES + 1, every, LANES), jnp.bfloat16),
            pltpu.VMEM((STEP * every, width), jnp.bfloat16),
            pltpu.VMEM((width, STEP * every), jnp.bfloat16),
            pltpu.VMEM((n_tm * n_sub, piece_rows, LANES), jnp.float32),
            pltpu.VMEM((group - 1, piece_rows, LANES), jnp.float32),
            pltpu.SemaphoreType.DMA((4,)),
            pltpu.SemaphoreType.DMA((2,)),
            pltpu.SemaphoreType.DMA((n_tm,)),
            pltpu.SemaphoreType.DMA((n_tm,)),
            pltpu.SemaphoreType.DMA((n_tm,)),
            pltpu.SemaphoreType.DMA((n_tm,)),
            pltpu.SemaphoreType.DMA((2,)),
        ],
        compiler_params=pltpu.CompilerParams(
            collective_id=0, has_side_effects=True, vmem_limit_bytes=60 * 2**20
        ),
    )(tile_list, archive, tail, precision)
    return out.reshape(-1)


def solution(mesh):
    placed = (P("ch", ("grp", "tm")), P(None, "grp"), P(), P(("grp", "tm"), "sub", None, None))
    return jax.shard_map(
        body, mesh=mesh, in_specs=placed, out_specs=P(("grp", "tm", "sub")), check_vma=False
    )
```

```python
import functools

import jax
import jax.numpy as jnp
from jax import lax
from jax.experimental import pallas as pl
from jax.experimental.pallas import tpu as pltpu
from jax.sharding import PartitionSpec as P

M = 128
TS = 512
SLOTS = 2
DEPTH = 2048
EXCL = 32
LANES = 128
STEP = 16
COLS = TS + M
ROWS = TS // 2 + M
SPAN = COLS + ROWS
MESH = pl.DeviceIdType.MESH


def whiten(factor, samples):
    return jnp.dot(
        factor, samples, precision=lax.Precision.HIGHEST, preferred_element_type=jnp.float32
    ).astype(jnp.bfloat16)


def kernel(
    n_tm,
    n_sub,
    tiles_hbm,
    archive_ref,
    tail_hbm,
    precision_hbm,
    out_ref,
    tiles_ref,
    tail_ref,
    precision_ref,
    raw_ref,
    series_ref,
    hankel_ref,
    lagged_ref,
    mine_ref,
    pair_ref,
    merged_ref,
    theirs_ref,
    load_sems,
    raw_sems,
    time_send,
    time_recv,
    pair_send,
    pair_recv,
    merge_sems,
    min_sems,
):
    tm, sub, ch = lax.axis_index("tm"), lax.axis_index("sub"), lax.axis_index("ch")
    other = 1 - ch
    group = n_tm * n_sub
    me = tm * n_sub + sub
    channels, span = archive_ref.shape
    half = span // 2
    starts_all = n_tm * span

    def crossed(a, b, count):
        total, bit = 0, 1
        while bit < count:
            total = total + lax.rem(a // bit + b // bit, 2) * bit
            bit *= 2
        return total

    def place(owner):
        return {"tm": owner // n_sub, "sub": owner % n_sub}

    def each_peer(action):
        if group <= 16:
            for step in reversed(range(1, group)):
                action(step)
        else:
            lax.fori_loop(1, group, lambda step, _: (action(group - step), 0)[1], 0)

    own_rows = pl.ds(pl.multiple_of(ch * channels, channels), channels)
    own_half = archive_ref.at[:, pl.ds(pl.multiple_of(ch * half, half), half)]
    loads = [
        pltpu.make_async_copy(source, target, load_sems.at[at])
        for at, (source, target) in enumerate(
            (
                (precision_hbm, precision_ref),
                (tail_hbm, tail_ref),
                (own_half, raw_ref.at[own_rows, :]),
                (tiles_hbm, tiles_ref),
            )
        )
    ]
    for load in loads:
        load.start()
    barrier = pltpu.get_barrier_semaphore()
    each_peer(
        lambda step: pl.semaphore_signal(
            barrier, inc=1, device_id=place(crossed(me, step, group)), device_id_type=MESH
        )
    )
    pl.semaphore_signal(barrier, inc=1, device_id={"ch": other}, device_id_type=MESH)
    for load in loads[:2]:
        load.wait()
    factor = precision_ref[...]
    last = starts_all // LANES
    series_ref[last] = jnp.zeros((2 * channels, LANES), jnp.bfloat16)
    series_ref[last, :, : M - 1] = whiten(factor, tail_ref[...])
    pl.semaphore_wait(barrier, group)

    swap = pltpu.make_async_remote_copy(
        src_ref=archive_ref.at[:, pl.ds(pl.multiple_of(other * half, half), half)],
        dst_ref=raw_ref.at[own_rows, :],
        send_sem=raw_sems.at[0],
        recv_sem=raw_sems.at[1],
        device_id={"ch": other},
        device_id_type=MESH,
    )
    swap.start()
    for load in loads[2:]:
        load.wait()
    swap.wait_recv()

    tiles = half // LANES

    def chunk(owner, part):
        return series_ref.at[pl.ds((owner * 2 + part) * tiles, tiles)]

    mine = chunk(tm, ch)
    whitened = whiten(factor, raw_ref[...])
    for k in range(tiles):
        series_ref[(tm * 2 + ch) * tiles + k] = whitened[:, k * LANES : (k + 1) * LANES]
    along_time = [None] * n_tm
    for far in sorted(range(1, n_tm), key=lambda d: (d < n_tm // 2, d)):
        along_time[far] = pltpu.make_async_remote_copy(
            src_ref=mine,
            dst_ref=mine,
            send_sem=time_send.at[far],
            recv_sem=time_recv.at[far],
            device_id={"tm": crossed(tm, far, n_tm)},
            device_id_type=MESH,
        )
        along_time[far].start()
    to_pair = []
    for far in range(n_tm):
        if far:
            along_time[far].wait_recv()
        held = chunk(crossed(tm, far, n_tm), ch)
        to_pair.append(
            pltpu.make_async_remote_copy(
                src_ref=held,
                dst_ref=held,
                send_sem=pair_send.at[far],
                recv_sem=pair_recv.at[far],
                device_id={"ch": other},
                device_id_type=MESH,
            )
        )
        to_pair[far].start()
    for copy in to_pair:
        copy.wait_recv()

    pieces = []
    for slot in range(SLOTS):
        per_block = TS // LANES
        row_tile = tiles_ref[0, 0, slot, 0] * per_block + ch * (per_block // 2)
        col_tile = tiles_ref[0, 0, slot, 1] * per_block
        pieces.extend(series_ref[col_tile + k] for k in range(COLS // LANES))
        pieces.extend(series_ref[row_tile + k] for k in range(ROWS // LANES))
    segment = jnp.concatenate(pieces, axis=1).astype(jnp.float32)
    width = segment.shape[1]
    depth = segment.shape[0]
    for lag in range(STEP):
        moved = segment if lag == 0 else pltpu.roll(segment, width - lag, axis=1)
        hankel_ref[lag * depth : (lag + 1) * depth, :] = moved.astype(jnp.bfloat16)
    size = STEP * depth
    unit = (
        lax.broadcasted_iota(jnp.int32, (size, size), 0)
        == lax.broadcasted_iota(jnp.int32, (size, size), 1)
    ).astype(jnp.bfloat16)
    for at in range(0, width, size):
        lagged_ref[at : at + size, :] = lax.dot_general(
            unit,
            hankel_ref[:, at : at + size],
            (((1,), (1,)), ((), ())),
            preferred_element_type=jnp.float32,
        ).astype(jnp.bfloat16)
    norms = jnp.broadcast_to(jnp.sum(segment * segment, axis=0, keepdims=True), (8, width))
    shift = 1
    while shift < M:
        norms = norms + pltpu.roll(norms, width - shift, axis=1)
        shift *= 2

    owners, piece_rows, _ = mine_ref.shape
    place_shape = (owners, piece_rows, LANES)
    line = lax.broadcasted_iota(jnp.int32, place_shape, 0) * piece_rows
    line = line + lax.broadcasted_iota(jnp.int32, place_shape, 1)
    block_of, part_of = line // per_block, line % per_block
    best = jnp.full(place_shape, jnp.inf, jnp.float32)
    for slot in range(SLOTS):
        col_at = slot * SPAN
        row_at = col_at + COLS
        n_rows = TS // 2
        left = jnp.concatenate(
            [lagged_ref[row_at + v : row_at + v + n_rows, :] for v in range(0, M, STEP)], axis=1
        )
        right = jnp.concatenate(
            [lagged_ref[col_at + v : col_at + v + TS, :] for v in range(0, M, STEP)], axis=1
        )
        products = lax.dot_general(
            left, right, (((1,), (1,)), ((), ())), preferred_element_type=jnp.float32
        )
        row_block = tiles_ref[0, 0, slot, 0]
        col_block = tiles_ref[0, 0, slot, 1]
        between = row_block * TS + ch * n_rows - col_block * TS
        separation = (
            lax.broadcasted_iota(jnp.int32, (n_rows, TS), 0)
            - lax.broadcasted_iota(jnp.int32, (n_rows, TS), 1)
            + between
        )
        scores = jnp.where(jnp.abs(separation) < EXCL, jnp.inf, -2.0 * products)
        row_norms = norms[:1, row_at : row_at + n_rows]
        col_norms = norms[:1, col_at : col_at + TS]
        row_wide = jnp.transpose(jnp.broadcast_to(row_norms, (LANES, n_rows)))
        by_col = jnp.min(scores + jnp.concatenate([row_wide] * per_block, axis=1), axis=0, keepdims=True)
        by_col = (by_col + col_norms) * (1.0 / DEPTH)
        with_col = scores + col_norms
        folded = with_col[:, :LANES]
        for q in range(1, per_block):
            folded = jnp.minimum(folded, with_col[:, q * LANES : (q + 1) * LANES])
        by_row = jnp.min(jnp.transpose(folded), axis=0, keepdims=True)
        by_row = (by_row + row_norms) * (1.0 / DEPTH)
        for q in range(per_block):
            here = by_col[:, q * LANES : (q + 1) * LANES].reshape(1, 1, LANES)
            hit = (block_of == col_block) & (part_of == q)
            best = jnp.minimum(best, jnp.where(hit, here, jnp.inf))
        for q in range(per_block // 2):
            here = by_row[:, q * LANES : (q + 1) * LANES].reshape(1, 1, LANES)
            hit = (block_of == row_block) & (part_of == q + ch * (per_block // 2))
            best = jnp.minimum(best, jnp.where(hit, here, jnp.inf))
    mine_ref[...] = best

    merge = pltpu.make_async_remote_copy(
        src_ref=mine_ref,
        dst_ref=pair_ref,
        send_sem=merge_sems.at[0],
        recv_sem=merge_sems.at[1],
        device_id={"ch": other},
        device_id_type=MESH,
    )
    merge.start()
    merge.wait_recv()
    merged_ref[...] = jnp.minimum(best, pair_ref[...])

    def send_minima(step):
        owner = crossed(me, step, group)
        pltpu.make_async_remote_copy(
            src_ref=merged_ref.at[owner],
            dst_ref=theirs_ref.at[step - 1],
            send_sem=min_sems.at[0],
            recv_sem=min_sems.at[1],
            device_id=place(owner),
            device_id_type=MESH,
        ).start()

    each_peer(send_minima)
    every = pltpu.make_async_remote_copy(
        src_ref=theirs_ref,
        dst_ref=theirs_ref,
        send_sem=min_sems.at[0],
        recv_sem=min_sems.at[1],
        device_id={"ch": other},
        device_id_type=MESH,
    )
    every.wait_recv()
    out_ref[...] = jnp.minimum(merged_ref[me], jnp.min(theirs_ref[...], axis=0))
    merge.wait_send()
    every.wait_send()
    swap.wait_send()
    for copy in along_time[1:] + to_pair:
        copy.wait_send()


def body(archive, tail, precision, tile_list):
    n_tm, n_sub = lax.axis_size("tm"), lax.axis_size("sub")
    group = n_tm * n_sub
    channels, span = archive.shape
    starts_all = span * n_tm
    piece_rows = starts_all // (n_tm * n_sub) // LANES
    every = 2 * channels
    width = SLOTS * SPAN
    anywhere = pl.BlockSpec(memory_space=pl.ANY)
    out = pl.pallas_call(
        functools.partial(kernel, n_tm, n_sub),
        out_shape=jax.ShapeDtypeStruct((piece_rows, LANES), jnp.float32),
        in_specs=[anywhere] * 4,
        out_specs=pl.BlockSpec(memory_space=pltpu.VMEM),
        scratch_shapes=[
            pltpu.SMEM(tile_list.shape, jnp.int32),
            pltpu.VMEM(tail.shape, jnp.float32),
            pltpu.VMEM(precision.shape, jnp.float32),
            pltpu.VMEM((every, span // 2), jnp.float32),
            pltpu.VMEM((starts_all // LANES + 1, every, LANES), jnp.bfloat16),
            pltpu.VMEM((STEP * every, width), jnp.bfloat16),
            pltpu.VMEM((width, STEP * every), jnp.bfloat16),
            pltpu.VMEM((group, piece_rows, LANES), jnp.float32),
            pltpu.VMEM((group, piece_rows, LANES), jnp.float32),
            pltpu.VMEM((group, piece_rows, LANES), jnp.float32),
            pltpu.VMEM((group - 1, piece_rows, LANES), jnp.float32),
            pltpu.SemaphoreType.DMA((4,)),
            pltpu.SemaphoreType.DMA((2,)),
            pltpu.SemaphoreType.DMA((n_tm,)),
            pltpu.SemaphoreType.DMA((n_tm,)),
            pltpu.SemaphoreType.DMA((n_tm,)),
            pltpu.SemaphoreType.DMA((n_tm,)),
            pltpu.SemaphoreType.DMA((2,)),
            pltpu.SemaphoreType.DMA((2,)),
        ],
        compiler_params=pltpu.CompilerParams(
            collective_id=0, has_side_effects=True, vmem_limit_bytes=60 * 2**20
        ),
    )(tile_list, archive, tail, precision)
    return out.reshape(-1)


def solution(mesh):
    placed = (P("ch", ("grp", "tm")), P(None, "grp"), P(), P(("grp", "tm"), "sub", None, None))
    return jax.shard_map(
        body, mesh=mesh, in_specs=placed, out_specs=P(("grp", "tm", "sub")), check_vma=False
    )
```

```python
import functools

import jax
import jax.numpy as jnp
from jax import lax
from jax.experimental import pallas as pl
from jax.experimental.pallas import tpu as pltpu
from jax.sharding import PartitionSpec as P

M = 128
TS = 512
SLOTS = 2
DEPTH = 2048
EXCL = 32
LANES = 128
STEP = 16
COLS = TS + M
ROWS = TS // 2 + M
SPAN = COLS + ROWS
MESH = pl.DeviceIdType.MESH


def whiten(factor, samples):
    return jnp.dot(
        factor, samples, precision=lax.Precision.HIGHEST, preferred_element_type=jnp.float32
    ).astype(jnp.bfloat16)


def kernel(
    n_tm,
    n_sub,
    tiles_hbm,
    archive_ref,
    tail_hbm,
    precision_hbm,
    out_ref,
    tiles_ref,
    tail_ref,
    precision_ref,
    raw_ref,
    series_ref,
    hankel_ref,
    lagged_ref,
    mine_ref,
    theirs_ref,
    load_sems,
    raw_sems,
    time_send,
    time_recv,
    pair_send,
    pair_recv,
    min_sems,
):
    tm, sub, ch = lax.axis_index("tm"), lax.axis_index("sub"), lax.axis_index("ch")
    other = 1 - ch
    group = n_tm * n_sub * 2
    me = (tm * n_sub + sub) * 2 + ch
    channels, span = archive_ref.shape
    half = span // 2
    starts_all = n_tm * span

    def place(rank):
        owner = rank // 2
        return {"tm": owner // n_sub, "sub": owner % n_sub, "ch": rank % 2}

    def each_peer(action):
        if group <= 16:
            for step in range(1, group):
                action(step)
        else:
            lax.fori_loop(1, group, lambda step, _: (action(step), 0)[1], 0)

    own_rows = pl.ds(pl.multiple_of(ch * channels, channels), channels)
    own_half = archive_ref.at[:, pl.ds(pl.multiple_of(ch * half, half), half)]
    loads = [
        pltpu.make_async_copy(source, target, load_sems.at[at])
        for at, (source, target) in enumerate(
            (
                (precision_hbm, precision_ref),
                (tail_hbm, tail_ref),
                (own_half, raw_ref.at[own_rows, :]),
                (tiles_hbm, tiles_ref),
            )
        )
    ]
    for load in loads:
        load.start()
    barrier = pltpu.get_barrier_semaphore()
    each_peer(
        lambda step: pl.semaphore_signal(
            barrier, inc=1, device_id=place(lax.rem(me + step, group)), device_id_type=MESH
        )
    )
    for load in loads[:2]:
        load.wait()
    factor = precision_ref[...]
    last = starts_all // LANES
    series_ref[last] = jnp.zeros((2 * channels, LANES), jnp.bfloat16)
    series_ref[last, :, : M - 1] = whiten(factor, tail_ref[...])
    pl.semaphore_wait(barrier, group - 1)

    swap = pltpu.make_async_remote_copy(
        src_ref=archive_ref.at[:, pl.ds(pl.multiple_of(other * half, half), half)],
        dst_ref=raw_ref.at[own_rows, :],
        send_sem=raw_sems.at[0],
        recv_sem=raw_sems.at[1],
        device_id={"ch": other},
        device_id_type=MESH,
    )
    swap.start()
    for load in loads[2:]:
        load.wait()
    swap.wait_recv()

    tiles = half // LANES

    def chunk(owner, part):
        return series_ref.at[pl.ds((owner * 2 + part) * tiles, tiles)]

    mine = chunk(tm, ch)
    whitened = whiten(factor, raw_ref[...])
    for k in range(tiles):
        series_ref[(tm * 2 + ch) * tiles + k] = whitened[:, k * LANES : (k + 1) * LANES]
    along_time, to_pair = [None], []
    for back in range(n_tm):
        later = lax.rem(tm + back, n_tm)
        if back:
            along_time.append(
                pltpu.make_async_remote_copy(
                    src_ref=mine,
                    dst_ref=mine,
                    send_sem=time_send.at[back],
                    recv_sem=time_recv.at[back],
                    device_id={"tm": later},
                    device_id_type=MESH,
                )
            )
            along_time[back].start()
        to_pair.append(
            pltpu.make_async_remote_copy(
                src_ref=mine,
                dst_ref=mine,
                send_sem=pair_send.at[back],
                recv_sem=pair_recv.at[back],
                device_id={"tm": later, "ch": other},
                device_id_type=MESH,
            )
        )
        to_pair[back].start()
    for copy in along_time[1:]:
        copy.wait_recv()
    for copy in to_pair:
        copy.wait_recv()

    pieces = []
    for slot in range(SLOTS):
        per_block = TS // LANES
        row_tile = tiles_ref[0, 0, slot, 0] * per_block + ch * (per_block // 2)
        col_tile = tiles_ref[0, 0, slot, 1] * per_block
        pieces.extend(series_ref[col_tile + k] for k in range(COLS // LANES))
        pieces.extend(series_ref[row_tile + k] for k in range(ROWS // LANES))
    segment = jnp.concatenate(pieces, axis=1).astype(jnp.float32)
    width = segment.shape[1]
    depth = segment.shape[0]
    for lag in range(STEP):
        moved = segment if lag == 0 else pltpu.roll(segment, width - lag, axis=1)
        hankel_ref[lag * depth : (lag + 1) * depth, :] = moved.astype(jnp.bfloat16)
    size = STEP * depth
    unit = (
        lax.broadcasted_iota(jnp.int32, (size, size), 0)
        == lax.broadcasted_iota(jnp.int32, (size, size), 1)
    ).astype(jnp.bfloat16)
    for at in range(0, width, size):
        lagged_ref[at : at + size, :] = lax.dot_general(
            unit,
            hankel_ref[:, at : at + size],
            (((1,), (1,)), ((), ())),
            preferred_element_type=jnp.float32,
        ).astype(jnp.bfloat16)
    norms = jnp.broadcast_to(jnp.sum(segment * segment, axis=0, keepdims=True), (8, width))
    shift = 1
    while shift < M:
        norms = norms + pltpu.roll(norms, width - shift, axis=1)
        shift *= 2

    owners, piece_rows, _ = mine_ref.shape
    place_shape = (owners, piece_rows, LANES)
    line = lax.broadcasted_iota(jnp.int32, place_shape, 0) * piece_rows
    line = line + lax.broadcasted_iota(jnp.int32, place_shape, 1)
    block_of, part_of = line // per_block, line % per_block
    best = jnp.full(place_shape, jnp.inf, jnp.float32)
    for slot in range(SLOTS):
        col_at = slot * SPAN
        row_at = col_at + COLS
        n_rows = TS // 2
        left = jnp.concatenate(
            [lagged_ref[row_at + v : row_at + v + n_rows, :] for v in range(0, M, STEP)], axis=1
        )
        right = jnp.concatenate(
            [lagged_ref[col_at + v : col_at + v + TS, :] for v in range(0, M, STEP)], axis=1
        )
        products = lax.dot_general(
            left, right, (((1,), (1,)), ((), ())), preferred_element_type=jnp.float32
        )
        row_block = tiles_ref[0, 0, slot, 0]
        col_block = tiles_ref[0, 0, slot, 1]
        between = row_block * TS + ch * n_rows - col_block * TS
        separation = (
            lax.broadcasted_iota(jnp.int32, (n_rows, TS), 0)
            - lax.broadcasted_iota(jnp.int32, (n_rows, TS), 1)
            + between
        )
        scores = jnp.where(jnp.abs(separation) < EXCL, jnp.inf, -2.0 * products)
        row_norms = norms[:1, row_at : row_at + n_rows]
        col_norms = norms[:1, col_at : col_at + TS]
        row_wide = jnp.transpose(jnp.broadcast_to(row_norms, (LANES, n_rows)))
        by_col = jnp.min(scores + jnp.concatenate([row_wide] * per_block, axis=1), axis=0, keepdims=True)
        by_col = (by_col + col_norms) * (1.0 / DEPTH)
        with_col = scores + col_norms
        folded = with_col[:, :LANES]
        for q in range(1, per_block):
            folded = jnp.minimum(folded, with_col[:, q * LANES : (q + 1) * LANES])
        by_row = jnp.min(jnp.transpose(folded), axis=0, keepdims=True)
        by_row = (by_row + row_norms) * (1.0 / DEPTH)
        for q in range(per_block):
            here = by_col[:, q * LANES : (q + 1) * LANES].reshape(1, 1, LANES)
            hit = (block_of == col_block) & (part_of == q)
            best = jnp.minimum(best, jnp.where(hit, here, jnp.inf))
        for q in range(per_block // 2):
            here = by_row[:, q * LANES : (q + 1) * LANES].reshape(1, 1, LANES)
            hit = (block_of == row_block) & (part_of == q + ch * (per_block // 2))
            best = jnp.minimum(best, jnp.where(hit, here, jnp.inf))
    mine_ref[...] = best

    def send_minima(step):
        rank = lax.rem(me + step, group)
        pltpu.make_async_remote_copy(
            src_ref=mine_ref.at[rank // 2],
            dst_ref=theirs_ref.at[step - 1],
            send_sem=min_sems.at[0],
            recv_sem=min_sems.at[1],
            device_id=place(rank),
            device_id_type=MESH,
        ).start()

    each_peer(send_minima)
    every = pltpu.make_async_remote_copy(
        src_ref=theirs_ref,
        dst_ref=theirs_ref,
        send_sem=min_sems.at[0],
        recv_sem=min_sems.at[1],
        device_id={"ch": other},
        device_id_type=MESH,
    )
    every.wait_recv()
    out_ref[...] = jnp.minimum(mine_ref[me // 2], jnp.min(theirs_ref[...], axis=0))
    every.wait_send()
    swap.wait_send()
    for copy in along_time[1:] + to_pair:
        copy.wait_send()


def body(archive, tail, precision, tile_list):
    n_tm, n_sub = lax.axis_size("tm"), lax.axis_size("sub")
    group = n_tm * n_sub * 2
    channels, span = archive.shape
    starts_all = span * n_tm
    piece_rows = starts_all // (n_tm * n_sub) // LANES
    every = 2 * channels
    width = SLOTS * SPAN
    anywhere = pl.BlockSpec(memory_space=pl.ANY)
    out = pl.pallas_call(
        functools.partial(kernel, n_tm, n_sub),
        out_shape=jax.ShapeDtypeStruct((piece_rows, LANES), jnp.float32),
        in_specs=[anywhere] * 4,
        out_specs=pl.BlockSpec(memory_space=pltpu.VMEM),
        scratch_shapes=[
            pltpu.SMEM(tile_list.shape, jnp.int32),
            pltpu.VMEM(tail.shape, jnp.float32),
            pltpu.VMEM(precision.shape, jnp.float32),
            pltpu.VMEM((every, span // 2), jnp.float32),
            pltpu.VMEM((starts_all // LANES + 1, every, LANES), jnp.bfloat16),
            pltpu.VMEM((STEP * every, width), jnp.bfloat16),
            pltpu.VMEM((width, STEP * every), jnp.bfloat16),
            pltpu.VMEM((n_tm * n_sub, piece_rows, LANES), jnp.float32),
            pltpu.VMEM((group - 1, piece_rows, LANES), jnp.float32),
            pltpu.SemaphoreType.DMA((4,)),
            pltpu.SemaphoreType.DMA((2,)),
            pltpu.SemaphoreType.DMA((n_tm,)),
            pltpu.SemaphoreType.DMA((n_tm,)),
            pltpu.SemaphoreType.DMA((n_tm,)),
            pltpu.SemaphoreType.DMA((n_tm,)),
            pltpu.SemaphoreType.DMA((2,)),
        ],
        compiler_params=pltpu.CompilerParams(
            collective_id=0, has_side_effects=True, vmem_limit_bytes=60 * 2**20
        ),
    )(tile_list, archive, tail, precision)
    return out.reshape(-1)


def solution(mesh):
    placed = (P("ch", ("grp", "tm")), P(None, "grp"), P(), P(("grp", "tm"), "sub", None, None))
    return jax.shard_map(
        body, mesh=mesh, in_specs=placed, out_specs=P(("grp", "tm", "sub")), check_vma=False
    )
```
